32 devices in a mesh: groups: 2 (over y), ranks: 8 (over z, x), side: 2 (over core).
Axes of the slice: x: 2, y: 2, z: 4, core: 2. Of those that a mesh axis runs over, the one named last changes fastest.
Arguments:
- queries: bfloat16 [4096, 4096], P(('groups', 'ranks'), 'side'), parts along dimension 0, may hold values from -25 to 25
- keys: bfloat16 [512, 4096], P(('groups', 'ranks'), 'side'), parts along dimension 0, may hold values from -6 to 6
- values: bfloat16 [512, 4096], P(('groups', 'ranks'), 'side'), parts along dimension 0, may hold values from -96 to 96
- residual: bfloat16 [4096, 4096], P(('groups', 'ranks'), 'side'), parts along dimension 0, may hold values from -6 to 6
- merge_map: int32 [4096], P(('groups', 'ranks')), parts along dimension 0, may hold values from 0 to 31, as said below
- expert_ids: int32 [512, 2], P(('groups', 'ranks')), parts along dimension 0, may hold values from 0 to 3, all different within a row; in each aligned block of 32 rows (0 to 31, 32 to 63, ...) at most 32 rows name the same one
- gate_weights: float32 [512, 2], P(('groups', 'ranks')), parts along dimension 0, may hold values from 0.25 to 1
- norm_gain: bfloat16 [4096], P('side'), may hold values from 0.3984375 to 1.59375
- w_gate: bfloat16 [8, 4096, 768], P('ranks', 'side'), may hold values from -0.09375 to 0.09375
- w_up: bfloat16 [8, 4096, 768], P('ranks', 'side'), may hold values from -0.09375 to 0.09375
- w_down: bfloat16 [8, 768, 4096], P('ranks', None, 'side'), may hold values from -0.15625 to 0.15625
Outputs:
- layer_out: bfloat16 [4096, 4096], P(('groups', 'ranks'), 'side'), parts along dimension 0
The draws below stay inside these ranges and needn't reach their ends.
There are 2 independent parts, one for each index of `groups`. The reference program is written for one: setup_inputs(seed, part) draws one part's arguments, and reference() takes and returns one part's arrays. A program takes and returns all parts, laid end to end along the dimension named above; an argument that names none is the same for every part. Nothing has to cross between parts.
Inputs may be any that keep to these rules, and one draw needn't show every extreme that they name: `merge_map`: each merged token m of shard r (r * 32 <= m < (r + 1) * 32) is the group of one or more tokens of shard r. `expert_ids`: the 2 experts of a merged token differ; among the merged tokens of one shard (aligned blocks of 32) no expert is named more than 32 times.
All inputs are finite; a program needn't handle non-finite values.
Results may differ from the reference program's by a relative error of at most 0.0065.
The reference program's roundings to bfloat16 on the way count: a program that leaves them out, or rounds other values in their place, can miss the bound.
Values may be sent and summed in bfloat16 or wider, within the bound.
A program may use at most 128 MiB of HBM per device.

```python
import math
import jax
import jax.numpy as jnp
import numpy as np
from jax import lax

D = 4096
HEAD_DIM = 128
FF = 1536
TOP = 2
Q_DEV = 256
MRG_DEV = 32
EXPERTS = 4
CAP = 32
TOKENS = 2048
MERGED = 256
SLOTS = 256


def draw_queries(key, part):
    key = jax.random.fold_in(key, 11)
    values_drawn = jnp.clip(jax.random.normal(key, (TOKENS, D), jnp.float32), -6.0, 6.0)
    return values_drawn.astype(jnp.bfloat16)


def draw_keys(key, part):
    key = jax.random.fold_in(key, 12)
    values_drawn = jnp.clip(jax.random.normal(key, (MERGED, D), jnp.float32), -6.0, 6.0)
    return values_drawn.astype(jnp.bfloat16)


def draw_merge_map(key, part):
    key = jax.random.fold_in(key, 13)
    shard_keys = jax.random.split(key, TOKENS // Q_DEV)

    def one_shard(shard_key):
        order_key, pick_key = jax.random.split(shard_key)
        ordering = jax.random.permutation(order_key, Q_DEV)
        position_ids = jnp.arange(Q_DEV, dtype=jnp.int32)
        random_slots = jax.random.randint(pick_key, (Q_DEV,), 0, MRG_DEV, dtype=jnp.int32)
        chosen_slots = jnp.where(position_ids < MRG_DEV, position_ids, random_slots)
        return chosen_slots[jnp.argsort(ordering, stable=True)]
    return jax.vmap(one_shard)(shard_keys).reshape(TOKENS).astype(jnp.int32)


def level_of(stream_key, extent, cuts, smallest, top_value):
    gain, own = 1.0, jax.random.fold_in(stream_key, 6)
    for position, parts in cuts:
        heights = jnp.exp(jax.random.uniform(jax.random.fold_in(own, position), (parts,), jnp.float32, smallest / len(cuts), top_value / len(cuts)))
        gain = gain * jnp.repeat(heights, extent[position] // parts).reshape([-1 if axis == position else 1 for axis in range(len(extent))])
    return gain


def routed_block(stream_key, own, number, rows, amount, top, most, lean):
    order = jax.random.permutation(stream_key, amount)
    heavy_load, ordinary = portions_of(amount, rows * top, most, lean, True), portions_of(amount, rows * top, most, lean, False)
    places = jnp.arange(amount)

    def named(sizes, rotation):
        used = int((sizes > 0).sum())
        fixed = max(1, used // 4)
        moved = fixed + (places - fixed + rotation * (used - fixed)) % max(1, amount - fixed)
        return jnp.zeros((amount,), jnp.int32).at[order[jnp.where(places < fixed, places, moved)]].set(jnp.asarray(sizes, jnp.int32))

    sizes = jnp.where(number % 4 == 0, named(heavy_load, number // 4), named(ordinary, number - number // 4 - 1))
    mixed = jax.random.permutation(jax.random.fold_in(own, 3), amount)
    giver, taker = mixed[0:amount // 2 * 2:2], mixed[1:amount // 2 * 2:2]
    room = jnp.minimum(sizes[giver] - 1, most - sizes[taker]) // 2
    room = jnp.where((giver == order[0]) | (taker == order[0]) | (sizes[taker] == 0), 0, jnp.maximum(room, 0))
    moved = jax.random.randint(jax.random.fold_in(own, 4), (amount // 2,), 0, 1 << 20) % (room + 1)
    sizes = sizes.at[giver].add(-moved).at[taker].add(moved)
    items = jnp.searchsorted(jnp.cumsum(sizes), jnp.arange(rows * top), side="right").astype(jnp.int32)
    listing = items.reshape(top, rows).T
    listing = listing[jax.random.permutation(jax.random.fold_in(own, 1), rows)]
    rotation = jax.random.randint(jax.random.fold_in(own, 2), (rows, 1), 0, top)
    return jnp.take_along_axis(listing, (jnp.arange(top)[None, :] + rotation) % top, axis=1)


def portions_of(amount, total, reach, skew, full):
    loads = [(1 << 20) // math.isqrt(standing ** skew) + 1 for standing in range(1, amount + 1)]
    largest = reach if full else min(reach, max(-(-total // amount), total * loads[0] // sum(loads)))
    least = 1 if total - largest >= amount - 1 else 0
    holding, surplus = [largest] + [least] * (amount - 1), total - largest - least * (amount - 1)
    while surplus > 0:
        free = [i for i in range(1, amount) if holding[i] < largest] or [i for i in range(1, amount) if holding[i] < reach]
        whole, remaining = sum([loads[i] for i in free]), surplus
        for i in free:
            addition = min(reach - holding[i], max(1, remaining * loads[i] // whole), surplus)
            holding[i] = holding[i] + addition
            surplus = surplus - addition
    return np.array(holding)


def normal_values(stream_key, extent, width, most, shards=(), held_as=jnp.bfloat16):
    gain = level_of(stream_key, extent, shards, -0.22, 0.18) if shards else 1.0
    values = jax.random.normal(stream_key, extent, jnp.float32) * width * gain
    return jnp.minimum(jnp.maximum(values, -most), most).astype(held_as)


def setup_inputs(seed: int = 0, part: int = 0) -> dict:
    streams_of = jax.random.split(jax.random.key(seed), 12)
    own_keys = jax.random.split(jax.random.fold_in(streams_of[11], part), 12)
    queries = draw_queries(jax.random.fold_in(jax.random.fold_in(streams_of[11], part), 71), part)
    keys = draw_keys(jax.random.fold_in(jax.random.fold_in(streams_of[11], part), 71), part)
    values = normal_values(own_keys[2], (MERGED, D), 16.0, 96.0, ((0, 8), (1, 2)))
    residual = normal_values(own_keys[3], (TOKENS, D), 1.0, 6.0, ((0, 8), (1, 2)))
    merge_map = draw_merge_map(jax.random.fold_in(jax.random.fold_in(streams_of[11], part), 71), part)
    expert_ids_keys = jax.random.split(jax.random.fold_in(own_keys[5], 1), MERGED // MRG_DEV)
    expert_ids_turns = jax.random.permutation(jax.random.fold_in(own_keys[5], 3), MERGED // MRG_DEV)
    expert_ids = jax.vmap(lambda own, number: routed_block(jax.random.fold_in(own_keys[5], 2), own, number, MRG_DEV, EXPERTS, TOP, CAP, 2))(expert_ids_keys, expert_ids_turns).reshape((MERGED, TOP))
    gate_weights = jnp.clip(0.25 + 0.75 * jax.random.uniform(own_keys[6], (MERGED, TOP), jnp.float32) ** level_of(own_keys[6], (MERGED, TOP), ((0, 8),), -0.2, 0.2), 0.25, 1.0)
    norm_gain = jnp.clip(1.0 + 0.12 * jax.random.normal(streams_of[7], (D,), jnp.float32), 0.3984375, 1.59375).astype(jnp.bfloat16)
    w_gate = normal_values(streams_of[8], (EXPERTS * 2, D, FF // 2), D ** -0.5, 0.09375, ((0, 8), (1, 2)))
    w_up = normal_values(streams_of[9], (EXPERTS * 2, D, FF // 2), D ** -0.5, 0.09375, ((0, 8), (1, 2)))
    w_down = normal_values(streams_of[10], (EXPERTS * 2, FF // 2, D), FF ** -0.5, 0.15625, ((0, 8), (2, 2)))
    return dict(queries=queries, keys=keys, values=values, residual=residual, merge_map=merge_map, expert_ids=expert_ids, gate_weights=gate_weights, norm_gain=norm_gain, w_gate=w_gate, w_up=w_up, w_down=w_down)


def reference(queries, keys, values, residual, merge_map, expert_ids, gate_weights, norm_gain, w_gate, w_up, w_down):
    head_count = D // HEAD_DIM
    factor = 1.0 / math.sqrt(HEAD_DIM)
    positions = jnp.arange(TOKENS, dtype=jnp.int32)
    group_ids = (positions // Q_DEV * MRG_DEV + merge_map).astype(jnp.int32)
    member_counts = jax.ops.segment_sum(jnp.ones((TOKENS,), jnp.float32), group_ids, num_segments=MERGED)
    key_bias = jnp.log(member_counts).astype(jnp.bfloat16).astype(jnp.float32)
    query_heads = queries.reshape(TOKENS, head_count, HEAD_DIM).transpose(1, 0, 2)
    key_heads = keys.reshape(MERGED, head_count, HEAD_DIM).transpose(1, 0, 2)
    value_heads = values.reshape(MERGED, head_count, HEAD_DIM).transpose(1, 0, 2)

    def one_head(operands):
        query_block, key_block, value_block = operands
        scores = jnp.dot(query_block, key_block.T, preferred_element_type=jnp.float32) * factor + key_bias[None, :]
        weights = jnp.exp(scores - lax.optimization_barrier(jnp.max(scores, axis=1, keepdims=True)))
        totals = lax.optimization_barrier(jnp.sum(weights, axis=1, keepdims=True))
        return jnp.dot(weights.astype(jnp.bfloat16), value_block, preferred_element_type=jnp.float32) / totals
    attended = lax.map(one_head, (query_heads, key_heads, value_heads))
    attended = attended.transpose(1, 0, 2).reshape(TOKENS, D)
    summed = residual.astype(jnp.float32) + attended
    merged_state = jax.ops.segment_sum(summed, group_ids, num_segments=MERGED) / member_counts[:, None]
    inverse = lax.rsqrt(lax.optimization_barrier(jnp.sum(merged_state * merged_state, axis=1)) / D + 1e-06)
    normed = (merged_state * inverse[:, None] * norm_gain.astype(jnp.float32)[None, :]).astype(jnp.bfloat16)
    flat_ids = expert_ids.reshape(-1)
    flat_gates = gate_weights.reshape(-1)

    def one_expert(expert_index):
        matches = flat_ids == expert_index
        found_pairs = jnp.nonzero(matches, size=SLOTS, fill_value=0)[0].astype(jnp.int32)
        valid_rows = (jnp.arange(SLOTS, dtype=jnp.int32) < jnp.sum(matches.astype(jnp.int32))).astype(jnp.float32)
        owner_rows = (found_pairs // TOP).astype(jnp.int32)
        chosen_rows = normed[owner_rows]
        gate_full = jnp.concatenate([w_gate[2 * expert_index], w_gate[2 * expert_index + 1]], axis=1)
        up_full = jnp.concatenate([w_up[2 * expert_index], w_up[2 * expert_index + 1]], axis=1)
        down_full = jnp.concatenate([w_down[2 * expert_index], w_down[2 * expert_index + 1]], axis=0)
        gate_proj = jnp.dot(chosen_rows, gate_full, preferred_element_type=jnp.float32)
        up_proj = jnp.dot(chosen_rows, up_full, preferred_element_type=jnp.float32)
        hidden = (jax.nn.silu(gate_proj) * up_proj).astype(jnp.bfloat16)
        result = jnp.dot(hidden, down_full, preferred_element_type=jnp.float32)
        return (owner_rows, result * (flat_gates[found_pairs] * valid_rows)[:, None])
    owners, results = lax.map(one_expert, jnp.arange(EXPERTS, dtype=jnp.int32))
    expert_out = jnp.zeros((MERGED, D), jnp.float32).at[owners.reshape(-1)].add(results.reshape(-1, D))
    return (summed + expert_out[group_ids]).astype(jnp.bfloat16)
```

```python
import functools
import math

import jax
import jax.numpy as jnp
from jax import lax
from jax.experimental import pallas as pl
from jax.experimental.pallas import tpu as pltpu
from jax.sharding import PartitionSpec as P

D = 4096
HEAD_DIM = 128
TOP = 2


CHUNK = 512


def local(
    queries,
    keys,
    values,
    residual,
    merge_map,
    expert_ids,
    gate_weights,
    norm_gain,
    w_gate,
    w_up,
    w_down,
):
    query_rows, half_width = queries.shape
    head_count = half_width // HEAD_DIM
    merged_rows = keys.shape[0]
    factor = 1.0 / math.sqrt(HEAD_DIM)
    members = (merge_map[:, None] == jnp.arange(merged_rows, dtype=jnp.int32)[None, :]).astype(
        jnp.float32
    )
    member_counts = jnp.sum(members, axis=0)
    key_bias = jnp.log(member_counts).astype(jnp.bfloat16)
    query_heads = queries.reshape(query_rows, head_count, HEAD_DIM)
    all_keys, all_values, all_bias = (
        lax.all_gather(keys, "ranks", axis=0, tiled=True),
        lax.all_gather(values, "ranks", axis=0, tiled=True),
        lax.all_gather(key_bias, "ranks", axis=0, tiled=True),
    )
    count_rows = all_keys.shape[0]
    scores = jnp.einsum(
        "qhd,khd->hqk",
        query_heads,
        all_keys.reshape(count_rows, head_count, HEAD_DIM),
        preferred_element_type=jnp.float32,
    )
    scores = scores * factor + all_bias.astype(jnp.float32)[None, None, :]
    weights = jnp.exp(scores - jnp.max(scores, axis=2, keepdims=True))
    totals = jnp.sum(weights, axis=2)
    weighted_sum = jnp.einsum(
        "hqk,khd->hqd",
        weights.astype(jnp.bfloat16),
        all_values.reshape(-1, head_count, HEAD_DIM),
        preferred_element_type=jnp.float32,
    )
    attended = (
        (weighted_sum / totals[:, :, None]).transpose(1, 0, 2).reshape(query_rows, half_width)
    )
    summed = residual.astype(jnp.float32) + attended
    merged_state = (
        jnp.dot(members.T, summed, precision=lax.Precision.HIGHEST) / member_counts[:, None]
    )
    square_sum = lax.psum(jnp.sum(merged_state * merged_state, axis=1), "side")
    inverse = lax.rsqrt(square_sum / D + 1e-06)
    normed = (merged_state * inverse[:, None] * norm_gain.astype(jnp.float32)[None, :]).astype(
        jnp.bfloat16
    )
    rank_total = lax.axis_size("ranks")
    expert_count = rank_total // 2
    capacity = max(2, 4 * merged_rows // expert_count)
    slot_count = rank_total * capacity
    flat_ids = expert_ids.reshape(-1)
    onehot = (flat_ids[:, None] == jnp.arange(expert_count, dtype=jnp.int32)[None, :]).astype(
        jnp.int32
    )
    position = jnp.sum((jnp.cumsum(onehot, axis=0) - 1) * onehot, axis=1)
    targets = (
        2 * flat_ids[:, None] + jnp.arange(2, dtype=jnp.int32)[None, :]
    ) * capacity + position[:, None]
    slot_hits = (
        jnp.arange(slot_count, dtype=jnp.int32)[:, None, None] == targets[None, :, :]
    ).astype(jnp.float32)
    routed = jnp.sum(slot_hits, axis=2).reshape(slot_count, merged_rows, TOP)
    spread = jnp.sum(routed, axis=2).astype(jnp.bfloat16)
    outgoing = jnp.dot(spread, normed, preferred_element_type=jnp.float32).astype(jnp.bfloat16)
    combine = jnp.einsum("tmk,mk->mt", routed, gate_weights, precision=lax.Precision.HIGHEST)
    incoming = lax.all_to_all(
        outgoing.reshape(rank_total, capacity, half_width),
        "ranks",
        split_axis=0,
        concat_axis=0,
        tiled=True,
    )
    incoming = incoming.reshape(slot_count, half_width)
    gate_part = jnp.dot(incoming, w_gate[0], preferred_element_type=jnp.float32)
    up_part = jnp.dot(incoming, w_up[0], preferred_element_type=jnp.float32)
    gate_proj, up_proj = (
        lax.psum(gate_part.astype(jnp.bfloat16), "side").astype(jnp.float32),
        lax.psum(up_part.astype(jnp.bfloat16), "side").astype(jnp.float32),
    )
    hidden = (jax.nn.silu(gate_proj) * up_proj).astype(jnp.bfloat16)
    partial_out = jnp.dot(hidden, w_down[0], preferred_element_type=jnp.float32)
    returned = lax.all_to_all(
        partial_out.reshape(rank_total, capacity, half_width).astype(jnp.bfloat16),
        "ranks",
        split_axis=0,
        concat_axis=0,
        tiled=True,
    ).astype(jnp.float32)
    expert_out = jnp.dot(
        combine, returned.reshape(slot_count, half_width), precision=lax.Precision.HIGHEST
    )
    layer_out = summed + jnp.dot(members, expert_out, precision=lax.Precision.HIGHEST)
    return layer_out.astype(jnp.bfloat16)


BF16 = jnp.bfloat16
F32 = jnp.float32
COLUMNS = 2


def dot(a, b, contract=((1,), (0,))):
    return lax.dot_general(a, b, (contract, ((), ())), preferred_element_type=F32)


def split_dot(a, b, contract=((1,), (0,))):
    high = b.astype(BF16)
    low = (b - high.astype(F32)).astype(BF16)
    return dot(a, high, contract) + dot(a, low, contract)


def layer_kernel(
    ranks,
    chunks,
    q_hbm,
    res_hbm,
    k_ref,
    v_ref,
    map_ref,
    ids_ref,
    gates_ref,
    gain_ref,
    wg_hbm,
    wu_hbm,
    wd_hbm,
    out_hbm,
    q_ref,
    res_ref,
    wg_ref,
    wu_ref,
    wd_ref,
    out_ref,
    kv,
    rows_all,
    misc,
    squares,
    square_pair,
    summed,
    gate_acc,
    up_acc,
    pair_out,
    pair_in,
    part,
    x_out,
    x_in,
    z_out,
    z_in,
    local_sem,
    out_sem,
    kv_send,
    kv_recv,
    row_send,
    row_recv,
    misc_send,
    misc_recv,
    sq_send,
    sq_recv,
    pair_send,
    pair_recv,
    x_send,
    x_recv,
    z_send,
    z_recv,
):
    me = lax.axis_index("ranks")
    side = lax.axis_index("side")
    line = ranks // COLUMNS
    z, x = me // COLUMNS, lax.rem(me, COLUMNS)
    merged = k_ref.shape[0]
    tokens, half = q_hbm.shape
    width = half // chunks
    slots = ranks * merged
    factor = 1.0 / math.sqrt(HEAD_DIM)

    def rank_at(dz):
        return lax.rem(z + dz + line, line) * COLUMNS + x

    across = z * COLUMNS + (1 - x)

    def remote(src, dst, send, recv, target):
        return pltpu.make_async_remote_copy(
            src_ref=src,
            dst_ref=dst,
            send_sem=send,
            recv_sem=recv,
            device_id=target,
            device_id_type=pl.DeviceIdType.MESH,
        )

    loads = [
        pltpu.make_async_copy(src, dst, local_sem.at[i])
        for i, (src, dst) in enumerate(
            [
                (q_hbm, q_ref),
                (res_hbm, res_ref),
                (wg_hbm, wg_ref),
                (wu_hbm, wu_ref),
                (wd_hbm, wd_ref),
            ]
        )
    ]

    barrier = pltpu.get_barrier_semaphore()
    for dz in range(1, line):
        pl.semaphore_signal(
            barrier, inc=1, device_id={"ranks": rank_at(dz)}, device_id_type=pl.DeviceIdType.MESH
        )
    pl.semaphore_signal(
        barrier, inc=1, device_id={"ranks": across}, device_id_type=pl.DeviceIdType.MESH
    )
    pl.semaphore_signal(
        barrier, inc=1, device_id={"side": 1 - side}, device_id_type=pl.DeviceIdType.MESH
    )

    for c in range(chunks):
        cols = slice(c * width, (c + 1) * width)
        kv[me, c, 0:merged, :] = k_ref[:, cols]
        kv[me, c, merged : 2 * merged, :] = v_ref[:, cols]

    def own_copies(view, send, recv):
        copies = [
            remote(view(me), view(me), send(dz - 1), recv(dz - 1), {"ranks": rank_at(dz)})
            for dz in range(1, line)
        ]
        copies.append(
            remote(view(me), view(me), send(line - 1), recv(line - 1), {"ranks": across})
        )
        return copies

    def forward(view, send, recv, dz):
        came = view(rank_at(-dz))
        return remote(came, came, send(line - 1 + dz), recv(line - 1 + dz), {"ranks": across})

    def arrival(view, recv, send, dz):
        came = view(rank_at(-dz))
        return remote(came, came, send(dz - 1), recv(dz - 1), {"ranks": rank_at(dz)})

    def crossed(view, recv, send, dz):
        came = view(lax.rem(z - dz + line, line) * COLUMNS + (1 - x))
        return remote(came, came, send(line - 1 + dz), recv(line - 1 + dz), {"ranks": across})

    def spread(view, send, recv):
        for copy in own_copies(view, send, recv):
            copy.start()

    def pass_on(view, send, recv):
        for dz in range(1, line):
            arrival(view, recv, send, dz).wait_recv()
            forward(view, send, recv, dz).start()

    def complete(view, send, recv):
        for dz in range(line):
            crossed(view, recv, send, dz).wait_recv()

    def finish(view, send, recv):
        for copy in own_copies(view, send, recv):
            copy.wait_send()
        for dz in range(1, line):
            forward(view, send, recv, dz).wait_send()

    def net(ref, send, recv, c=None):
        if c is None:
            return (lambda r: ref.at[r]), (lambda i: send.at[i]), (lambda i: recv.at[i])
        return (lambda r: ref.at[r, c]), (lambda i: send.at[c, i]), (lambda i: recv.at[c, i])

    kv_net = [net(kv, kv_send, kv_recv, c) for c in range(chunks)]
    row_net = [net(rows_all, row_send, row_recv, c) for c in range(chunks)]
    misc_net = net(misc, misc_send, misc_recv)
    sq_net = net(squares, sq_send, sq_recv)

    token_group = map_ref[...]
    members = (
        lax.broadcasted_iota(jnp.int32, (merged, tokens), 0) == token_group
    ).astype(F32)
    counts = jnp.sum(members, axis=1, keepdims=True)
    members = members.astype(BF16)
    own_lane = lax.broadcasted_iota(
        jnp.int32, (merged, slots), 0
    ) + me * merged == lax.broadcasted_iota(jnp.int32, (merged, slots), 1)

    def as_row(column):
        return jnp.sum(jnp.where(own_lane, column, 0.0), axis=0, keepdims=True)

    row_id = lax.broadcasted_iota(jnp.int32, (8, slots), 0)
    table = jnp.where(row_id == 7, as_row(jnp.log(counts).astype(BF16).astype(F32)), 0.0)
    ids, gates = ids_ref[...], gates_ref[...]
    for e in range(ranks // 2):
        share = jnp.sum(jnp.where(ids == e, gates, 0.0), axis=1, keepdims=True)
        table = table + jnp.where(row_id == e, as_row(share), 0.0)
    misc[me] = table

    pl.semaphore_wait(barrier, line + 1)
    spread(*kv_net[0])
    spread(*misc_net)
    for c in range(1, chunks):
        spread(*kv_net[c])
    for load in loads:
        load.start()

    pass_on(*misc_net)
    pass_on(*kv_net[0])
    complete(*misc_net)
    everything = jnp.sum(misc[...], axis=0)
    bias = everything[7:8, :]
    diagonal = lax.broadcasted_iota(jnp.int32, (slots, slots), 0) == lax.broadcasted_iota(
        jnp.int32, (slots, slots), 1
    )

    def as_column(row):
        return jnp.sum(jnp.where(diagonal, row, 0.0), axis=1, keepdims=True)

    my_share = as_column(
        jnp.sum(jnp.where(row_id == me // 2, everything, 0.0), axis=0, keepdims=True)
    )

    loads[0].wait()
    loads[1].wait()
    square_sum = jnp.zeros((merged, 1), F32)

    def project(c):
        complete(*row_net[c])
        inputs = rows_all[:, c].reshape(slots, width)
        along = slice(c * width, (c + 1) * width)
        gate = dot(inputs, wg_ref[along, :])
        up = dot(inputs, wu_ref[along, :])
        if c == 0:
            gate_acc[...] = gate
            up_acc[...] = up
        else:
            gate_acc[...] += gate
            up_acc[...] += up

    for c in range(chunks):
        if c + 1 < chunks:
            pass_on(*kv_net[c + 1])
        complete(*kv_net[c])
        for h in range(width // HEAD_DIM):
            inner = slice(h * HEAD_DIM, (h + 1) * HEAD_DIM)
            cols = slice(c * width + h * HEAD_DIM, c * width + (h + 1) * HEAD_DIM)
            key = kv[:, c, 0:merged, inner].reshape(slots, HEAD_DIM)
            value = kv[:, c, merged : 2 * merged, inner].reshape(slots, HEAD_DIM)
            scores = dot(q_ref[:, cols], key, ((1,), (1,))) * factor + bias
            probs = jnp.exp(scores - jnp.max(scores, axis=1, keepdims=True))
            total = jnp.sum(probs, axis=1, keepdims=True)
            attended = dot(probs.astype(BF16), value) / total
            summed[:, cols] = res_ref[:, cols].astype(F32) + attended
        cols = slice(c * width, (c + 1) * width)
        state = split_dot(members, summed[:, cols]) / counts
        square_sum = square_sum + jnp.sum(state * state, axis=1, keepdims=True)
        rows_all[me, c] = (state * gain_ref[:, cols].astype(F32)).astype(BF16)
        spread(*row_net[c])
        if c == chunks - 1:
            squares[me] = jnp.broadcast_to(as_row(square_sum), (8, slots))
            spread(*sq_net)
        if c == 1:
            loads[2].wait()
            loads[3].wait()
        if c >= 1:
            pass_on(*row_net[c - 1])
        if c >= 2:
            project(c - 2)

    pass_on(*row_net[chunks - 1])
    pass_on(*sq_net)
    project(chunks - 2)
    complete(*sq_net)
    square_pair[0] = jnp.sum(squares[...], axis=0)
    other = {"side": 1 - side}
    pair_copies = [
        remote(square_pair.at[0], square_pair.at[1], pair_send.at[2], pair_recv.at[2], other),
        remote(pair_out.at[0], pair_in.at[0], pair_send.at[0], pair_recv.at[0], other),
        remote(pair_out.at[1], pair_in.at[1], pair_send.at[1], pair_recv.at[1], other),
    ]
    pair_copies[0].start()
    project(chunks - 1)
    pair_out[0] = gate_acc[...].astype(BF16)
    pair_copies[1].start()
    pair_out[1] = up_acc[...].astype(BF16)
    pair_copies[2].start()
    pair_copies[0].wait_recv()
    all_squares = square_pair[0] + square_pair[1]
    inverse = as_column(lax.rsqrt(all_squares[0:1, :] / (2 * half) + 1e-06))
    pair_copies[1].wait_recv()
    gate = (gate_acc[...] + pair_in[0].astype(F32)) * inverse
    gate = gate / (1.0 + jnp.exp(-gate))
    pair_copies[2].wait_recv()
    hidden = (gate * ((up_acc[...] + pair_in[1].astype(F32)) * inverse)).astype(BF16)
    loads[4].wait()

    x_copies = [
        remote(x_out.at[c], x_in.at[c], x_send.at[c], x_recv.at[c], {"ranks": across})
        for c in range(chunks)
    ]
    z_copies = [
        [
            remote(
                z_out.at[c, dz - 1],
                z_in.at[c, dz - 1],
                z_send.at[c, dz - 1],
                z_recv.at[c, dz - 1],
                {"ranks": rank_at(dz)},
            )
            for dz in range(1, line)
        ]
        for c in range(chunks)
    ]

    def line_sums(c):
        x_copies[c].wait_recv()
        for dz in range(1, line):
            z_out[c, dz - 1] = (part[c, rank_at(dz)] + x_in[c, dz].astype(F32)).astype(BF16)
            z_copies[c][dz - 1].start()

    for c in range(chunks):
        cols = slice(c * width, (c + 1) * width)
        result = dot(hidden, wd_ref[:, cols]) * my_share
        part[c] = result.reshape(ranks, merged, width)
        for dz in range(line):
            there = lax.rem(z + dz, line) * COLUMNS + (1 - x)
            x_out[c, dz] = part[c, there].astype(BF16)
        x_copies[c].start()
    for c in range(chunks):
        line_sums(c)
    stores = []
    for c in range(chunks):
        cols = slice(c * width, (c + 1) * width)
        expert_out = part[c, me] + x_in[c, 0].astype(F32)
        for dz in range(1, line):
            z_copies[c][dz - 1].wait_recv()
            expert_out = expert_out + z_in[c, dz - 1].astype(F32)
        out_ref[:, cols] = (
            summed[:, cols] + split_dot(members, expert_out, ((0,), (0,)))
        ).astype(BF16)
        store = pltpu.make_async_copy(
            out_ref.at[:, pl.ds(c * width, width)],
            out_hbm.at[:, pl.ds(c * width, width)],
            out_sem.at[c],
        )
        store.start()
        stores.append(store)

    for c in range(chunks):
        finish(*kv_net[c])
        finish(*row_net[c])
        x_copies[c].wait_send()
        for copy in z_copies[c]:
            copy.wait_send()
    finish(*misc_net)
    finish(*sq_net)
    for copy in pair_copies:
        copy.wait_send()
    for store in stores:
        store.wait()


def fused(
    queries,
    keys,
    values,
    residual,
    merge_map,
    expert_ids,
    gate_weights,
    norm_gain,
    w_gate,
    w_up,
    w_down,
):
    ranks = lax.axis_size("ranks")
    tokens, half = queries.shape
    merged = keys.shape[0]
    hidden = w_gate.shape[2]
    chunks = half // CHUNK
    line = ranks // COLUMNS
    slots = ranks * merged
    vmem = pl.BlockSpec(memory_space=pltpu.VMEM)
    anywhere = pl.BlockSpec(memory_space=pl.ANY)
    dma = pltpu.SemaphoreType.DMA
    hops = 2 * line - 1
    return pl.pallas_call(
        functools.partial(layer_kernel, ranks, chunks),
        out_shape=jax.ShapeDtypeStruct((tokens, half), BF16),
        in_specs=[anywhere] * 2 + [vmem] * 6 + [anywhere] * 3,
        out_specs=anywhere,
        scratch_shapes=[
            pltpu.VMEM((tokens, half), BF16),
            pltpu.VMEM((tokens, half), BF16),
            pltpu.VMEM((half, hidden), BF16),
            pltpu.VMEM((half, hidden), BF16),
            pltpu.VMEM((hidden, half), BF16),
            pltpu.VMEM((tokens, half), BF16),
            pltpu.VMEM((ranks, chunks, 2 * merged, CHUNK), BF16),
            pltpu.VMEM((ranks, chunks, merged, CHUNK), BF16),
            pltpu.VMEM((ranks, 8, slots), F32),
            pltpu.VMEM((ranks, 8, slots), F32),
            pltpu.VMEM((2, 8, slots), F32),
            pltpu.VMEM((tokens, half), F32),
            pltpu.VMEM((slots, hidden), F32),
            pltpu.VMEM((slots, hidden), F32),
            pltpu.VMEM((2, slots, hidden), BF16),
            pltpu.VMEM((2, slots, hidden), BF16),
            pltpu.VMEM((chunks, ranks, merged, CHUNK), F32),
            pltpu.VMEM((chunks, line, merged, CHUNK), BF16),
            pltpu.VMEM((chunks, line, merged, CHUNK), BF16),
            pltpu.VMEM((chunks, line - 1, merged, CHUNK), BF16),
            pltpu.VMEM((chunks, line - 1, merged, CHUNK), BF16),
            dma((5,)),
            dma((chunks,)),
            dma((chunks, hops)),
            dma((chunks, hops)),
            dma((chunks, hops)),
            dma((chunks, hops)),
            dma((hops,)),
            dma((hops,)),
            dma((hops,)),
            dma((hops,)),
            dma((3,)),
            dma((3,)),
            dma((chunks,)),
            dma((chunks,)),
            dma((chunks, line - 1)),
            dma((chunks, line - 1)),
        ],
        compiler_params=pltpu.CompilerParams(
            collective_id=0, has_side_effects=True, vmem_limit_bytes=48 * 1024 * 1024
        ),
    )(
        queries,
        residual,
        keys,
        values,
        merge_map.reshape(1, tokens),
        expert_ids,
        gate_weights,
        norm_gain.reshape(1, half),
        w_gate[0],
        w_up[0],
        w_down[0],
    )


def layer(*arrays):
    ranks = lax.axis_size("ranks")
    merged, half = arrays[1].shape
    dense = 4 * merged // (ranks // 2) >= merged and ranks >= 4
    if dense and half % CHUNK == 0 and half // CHUNK >= 2:
        return fused(*arrays)
    return local(*arrays)


def solution(mesh):
    return jax.shard_map(
        layer,
        mesh=mesh,
        in_specs=(
            P(("groups", "ranks"), "side"),
            P(("groups", "ranks"), "side"),
            P(("groups", "ranks"), "side"),
            P(("groups", "ranks"), "side"),
            P(("groups", "ranks")),
            P(("groups", "ranks"), None),
            P(("groups", "ranks"), None),
            P("side"),
            P("ranks", "side", None),
            P("ranks", "side", None),
            P("ranks", None, "side"),
        ),
        out_specs=P(("groups", "ranks"), "side"),
        check_vma=False,
    )
```

```python
import functools
import math

import jax
import jax.numpy as jnp
from jax import lax
from jax.experimental import pallas as pl
from jax.experimental.pallas import tpu as pltpu
from jax.sharding import PartitionSpec as P

D = 4096
HEAD_DIM = 128
TOP = 2


CHUNK = 512
WINDOW = 1
SUM_WINDOW = 2


def local(
    queries,
    keys,
    values,
    residual,
    merge_map,
    expert_ids,
    gate_weights,
    norm_gain,
    w_gate,
    w_up,
    w_down,
):
    query_rows, half_width = queries.shape
    head_count = half_width // HEAD_DIM
    merged_rows = keys.shape[0]
    factor = 1.0 / math.sqrt(HEAD_DIM)
    members = (merge_map[:, None] == jnp.arange(merged_rows, dtype=jnp.int32)[None, :]).astype(
        jnp.float32
    )
    member_counts = jnp.sum(members, axis=0)
    key_bias = jnp.log(member_counts).astype(jnp.bfloat16)
    query_heads = queries.reshape(query_rows, head_count, HEAD_DIM)
    all_keys, all_values, all_bias = (
        lax.all_gather(keys, "ranks", axis=0, tiled=True),
        lax.all_gather(values, "ranks", axis=0, tiled=True),
        lax.all_gather(key_bias, "ranks", axis=0, tiled=True),
    )
    count_rows = all_keys.shape[0]
    scores = jnp.einsum(
        "qhd,khd->hqk",
        query_heads,
        all_keys.reshape(count_rows, head_count, HEAD_DIM),
        preferred_element_type=jnp.float32,
    )
    scores = scores * factor + all_bias.astype(jnp.float32)[None, None, :]
    weights = jnp.exp(scores - jnp.max(scores, axis=2, keepdims=True))
    totals = jnp.sum(weights, axis=2)
    weighted_sum = jnp.einsum(
        "hqk,khd->hqd",
        weights.astype(jnp.bfloat16),
        all_values.reshape(-1, head_count, HEAD_DIM),
        preferred_element_type=jnp.float32,
    )
    attended = (
        (weighted_sum / totals[:, :, None]).transpose(1, 0, 2).reshape(query_rows, half_width)
    )
    summed = residual.astype(jnp.float32) + attended
    merged_state = (
        jnp.dot(members.T, summed, precision=lax.Precision.HIGHEST) / member_counts[:, None]
    )
    square_sum = lax.psum(jnp.sum(merged_state * merged_state, axis=1), "side")
    inverse = lax.rsqrt(square_sum / D + 1e-06)
    normed = (merged_state * inverse[:, None] * norm_gain.astype(jnp.float32)[None, :]).astype(
        jnp.bfloat16
    )
    rank_total = lax.axis_size("ranks")
    expert_count = rank_total // 2
    capacity = max(2, 4 * merged_rows // expert_count)
    slot_count = rank_total * capacity
    flat_ids = expert_ids.reshape(-1)
    onehot = (flat_ids[:, None] == jnp.arange(expert_count, dtype=jnp.int32)[None, :]).astype(
        jnp.int32
    )
    position = jnp.sum((jnp.cumsum(onehot, axis=0) - 1) * onehot, axis=1)
    targets = (
        2 * flat_ids[:, None] + jnp.arange(2, dtype=jnp.int32)[None, :]
    ) * capacity + position[:, None]
    slot_hits = (
        jnp.arange(slot_count, dtype=jnp.int32)[:, None, None] == targets[None, :, :]
    ).astype(jnp.float32)
    routed = jnp.sum(slot_hits, axis=2).reshape(slot_count, merged_rows, TOP)
    spread = jnp.sum(routed, axis=2).astype(jnp.bfloat16)
    outgoing = jnp.dot(spread, normed, preferred_element_type=jnp.float32).astype(jnp.bfloat16)
    combine = jnp.einsum("tmk,mk->mt", routed, gate_weights, precision=lax.Precision.HIGHEST)
    incoming = lax.all_to_all(
        outgoing.reshape(rank_total, capacity, half_width),
        "ranks",
        split_axis=0,
        concat_axis=0,
        tiled=True,
    )
    incoming = incoming.reshape(slot_count, half_width)
    gate_part = jnp.dot(incoming, w_gate[0], preferred_element_type=jnp.float32)
    up_part = jnp.dot(incoming, w_up[0], preferred_element_type=jnp.float32)
    gate_proj, up_proj = (
        lax.psum(gate_part.astype(jnp.bfloat16), "side").astype(jnp.float32),
        lax.psum(up_part.astype(jnp.bfloat16), "side").astype(jnp.float32),
    )
    hidden = (jax.nn.silu(gate_proj) * up_proj).astype(jnp.bfloat16)
    partial_out = jnp.dot(hidden, w_down[0], preferred_element_type=jnp.float32)
    returned = lax.all_to_all(
        partial_out.reshape(rank_total, capacity, half_width).astype(jnp.bfloat16),
        "ranks",
        split_axis=0,
        concat_axis=0,
        tiled=True,
    ).astype(jnp.float32)
    expert_out = jnp.dot(
        combine, returned.reshape(slot_count, half_width), precision=lax.Precision.HIGHEST
    )
    layer_out = summed + jnp.dot(members, expert_out, precision=lax.Precision.HIGHEST)
    return layer_out.astype(jnp.bfloat16)


BF16 = jnp.bfloat16
F32 = jnp.float32
COLUMNS = 2


def dot(a, b, contract=((1,), (0,))):
    return lax.dot_general(a, b, (contract, ((), ())), preferred_element_type=F32)


def split_dot(a, b, contract=((1,), (0,))):
    high = b.astype(BF16)
    low = (b - high.astype(F32)).astype(BF16)
    return dot(a, high, contract) + dot(a, low, contract)


def layer_kernel(
    ranks,
    chunks,
    q_hbm,
    res_hbm,
    k_hbm,
    v_hbm,
    map_hbm,
    ids_hbm,
    gates_hbm,
    gain_hbm,
    wg_hbm,
    wu_hbm,
    wd_hbm,
    out_hbm,
    k_ref,
    v_ref,
    map_ref,
    ids_ref,
    gates_ref,
    gain_ref,
    q_ref,
    res_ref,
    wg_ref,
    wu_ref,
    wd_ref,
    out_ref,
    kv,
    rows_all,
    misc,
    squares,
    square_pair,
    summed,
    gate_acc,
    up_acc,
    pair_out,
    pair_in,
    part,
    x_out,
    x_in,
    z_out,
    z_in,
    local_sem,
    out_sem,
    kv_send,
    kv_recv,
    row_send,
    row_recv,
    misc_send,
    misc_recv,
    sq_send,
    sq_recv,
    pair_send,
    pair_recv,
    x_send,
    x_recv,
    z_send,
    z_recv,
):
    me = lax.axis_index("ranks")
    side = lax.axis_index("side")
    line = ranks // COLUMNS
    z, x = me // COLUMNS, lax.rem(me, COLUMNS)
    merged = k_hbm.shape[0]
    tokens, half = q_hbm.shape
    width = half // chunks
    slots = ranks * merged
    factor = 1.0 / math.sqrt(HEAD_DIM)

    def rank_at(dz):
        return lax.rem(z + dz + line, line) * COLUMNS + x

    across = z * COLUMNS + (1 - x)

    def remote(src, dst, send, recv, target):
        return pltpu.make_async_remote_copy(
            src_ref=src,
            dst_ref=dst,
            send_sem=send,
            recv_sem=recv,
            device_id=target,
            device_id_type=pl.DeviceIdType.MESH,
        )

    loads = [
        pltpu.make_async_copy(src, dst, local_sem.at[i])
        for i, (src, dst) in enumerate(
            [
                (q_hbm, q_ref),
                (res_hbm, res_ref),
                (wg_hbm, wg_ref),
                (wu_hbm, wu_ref),
                (wd_hbm, wd_ref),
                (k_hbm, k_ref),
                (v_hbm, v_ref),
                (map_hbm, map_ref),
                (ids_hbm, ids_ref),
                (gates_hbm, gates_ref),
                (gain_hbm, gain_ref),
            ]
        )
    ]

    for load in loads[5:]:
        load.start()

    barrier = pltpu.get_barrier_semaphore()
    for dz in range(1, line):
        pl.semaphore_signal(
            barrier, inc=1, device_id={"ranks": rank_at(dz)}, device_id_type=pl.DeviceIdType.MESH
        )
    pl.semaphore_signal(
        barrier, inc=1, device_id={"ranks": across}, device_id_type=pl.DeviceIdType.MESH
    )
    pl.semaphore_signal(
        barrier, inc=1, device_id={"side": 1 - side}, device_id_type=pl.DeviceIdType.MESH
    )

    loads[5].wait()
    loads[6].wait()
    for c in range(chunks):
        cols = slice(c * width, (c + 1) * width)
        kv[me, c, 0:merged, :] = k_ref[:, cols]
        kv[me, c, merged : 2 * merged, :] = v_ref[:, cols]

    def own_copies(view, send, recv):
        copies = [
            remote(view(me), view(me), send(dz - 1), recv(dz - 1), {"ranks": rank_at(dz)})
            for dz in range(1, line)
        ]
        copies.append(
            remote(view(me), view(me), send(line - 1), recv(line - 1), {"ranks": across})
        )
        return copies

    def forward(view, send, recv, dz):
        came = view(rank_at(-dz))
        return remote(came, came, send(line - 1 + dz), recv(line - 1 + dz), {"ranks": across})

    def arrival(view, recv, send, dz):
        came = view(rank_at(-dz))
        return remote(came, came, send(dz - 1), recv(dz - 1), {"ranks": rank_at(dz)})

    def crossed(view, recv, send, dz):
        came = view(lax.rem(z - dz + line, line) * COLUMNS + (1 - x))
        return remote(came, came, send(line - 1 + dz), recv(line - 1 + dz), {"ranks": across})

    def spread(view, send, recv):
        for copy in own_copies(view, send, recv):
            copy.start()

    def pass_on(view, send, recv):
        for dz in range(1, line):
            arrival(view, recv, send, dz).wait_recv()
            forward(view, send, recv, dz).start()

    def advance(c):
        pass_on(*kv_net[c])
        if c + WINDOW < chunks:
            spread(*kv_net[c + WINDOW])

    def complete(view, send, recv):
        for dz in range(line):
            crossed(view, recv, send, dz).wait_recv()

    def finish(view, send, recv):
        for copy in own_copies(view, send, recv):
            copy.wait_send()
        for dz in range(1, line):
            forward(view, send, recv, dz).wait_send()

    def net(ref, send, recv, c=None):
        if c is None:
            return (lambda r: ref.at[r]), (lambda i: send.at[i]), (lambda i: recv.at[i])
        return (lambda r: ref.at[r, c]), (lambda i: send.at[c, i]), (lambda i: recv.at[c, i])

    kv_net = [net(kv, kv_send, kv_recv, c) for c in range(chunks)]
    row_net = [net(rows_all, row_send, row_recv, c) for c in range(chunks)]
    misc_net = net(misc, misc_send, misc_recv)
    sq_net = net(squares, sq_send, sq_recv)

    pl.semaphore_wait(barrier, line + 1)
    for c in range(min(WINDOW, chunks)):
        spread(*kv_net[c])
    for load in loads[:5]:
        load.start()
    for load in loads[7:]:
        load.wait()
    token_group = map_ref[...]
    members = (
        lax.broadcasted_iota(jnp.int32, (merged, tokens), 0) == token_group
    ).astype(F32)
    counts = jnp.sum(members, axis=1, keepdims=True)
    members = members.astype(BF16)
    own_lane = lax.broadcasted_iota(
        jnp.int32, (merged, slots), 0
    ) + me * merged == lax.broadcasted_iota(jnp.int32, (merged, slots), 1)

    def as_row(column):
        return jnp.sum(jnp.where(own_lane, column, 0.0), axis=0, keepdims=True)

    row_id = lax.broadcasted_iota(jnp.int32, (8, slots), 0)
    square = lax.broadcasted_iota(jnp.int32, (merged, merged), 0) == lax.broadcasted_iota(
        jnp.int32, (merged, merged), 1
    )
    table = jnp.where(row_id == 7, as_row(jnp.log(counts).astype(BF16).astype(F32)), 0.0)
    ids, gates = ids_ref[...], gates_ref[...]
    for e in range(ranks // 2):
        share = jnp.sum(jnp.where(ids == e, gates, 0.0), axis=0, keepdims=True)
        share = jnp.sum(jnp.where(square, share, 0.0), axis=1, keepdims=True)
        table = table + jnp.where(row_id == e, as_row(share), 0.0)
    misc[me] = table

    spread(*misc_net)
    pass_on(*misc_net)
    advance(0)
    complete(*misc_net)
    everything = jnp.sum(misc[...], axis=0)
    bias = everything[7:8, :]
    diagonal = lax.broadcasted_iota(jnp.int32, (slots, slots), 0) == lax.broadcasted_iota(
        jnp.int32, (slots, slots), 1
    )

    def as_column(row):
        return jnp.sum(jnp.where(diagonal, row, 0.0), axis=1, keepdims=True)

    my_share = as_column(
        jnp.sum(jnp.where(row_id == me // 2, everything, 0.0), axis=0, keepdims=True)
    )

    loads[0].wait()
    loads[1].wait()
    square_sum = jnp.zeros((merged, 1), F32)
    heads = width // HEAD_DIM

    def gain_row(c):
        rows = [gain_ref[c * heads + h : c * heads + h + 1, :] for h in range(heads)]
        return jnp.concatenate(rows, axis=1).astype(F32)


    def project(c):
        complete(*row_net[c])
        inputs = rows_all[:, c].reshape(slots, width)
        along = slice(c * width, (c + 1) * width)
        gate = dot(inputs, wg_ref[along, :])
        up = dot(inputs, wu_ref[along, :])
        if c == 0:
            gate_acc[...] = gate
            up_acc[...] = up
        else:
            gate_acc[...] += gate
            up_acc[...] += up

    for c in range(chunks):
        if c + 1 < chunks:
            advance(c + 1)
        complete(*kv_net[c])
        for h in range(heads):
            inner = slice(h * HEAD_DIM, (h + 1) * HEAD_DIM)
            cols = slice(c * width + h * HEAD_DIM, c * width + (h + 1) * HEAD_DIM)
            key = kv[:, c, 0:merged, inner].reshape(slots, HEAD_DIM)
            value = kv[:, c, merged : 2 * merged, inner].reshape(slots, HEAD_DIM)
            scores = dot(q_ref[:, cols], key, ((1,), (1,))) * factor + bias
            probs = jnp.exp(scores - jnp.max(scores, axis=1, keepdims=True))
            total = jnp.sum(probs, axis=1, keepdims=True)
            attended = dot(probs.astype(BF16), value) / total
            summed[:, cols] = res_ref[:, cols].astype(F32) + attended
        cols = slice(c * width, (c + 1) * width)
        state = split_dot(members, summed[:, cols]) / counts
        square_sum = square_sum + jnp.sum(state * state, axis=1, keepdims=True)
        rows_all[me, c] = (state * gain_row(c)).astype(BF16)
        spread(*row_net[c])
        if c == chunks - 1:
            squares[me] = jnp.broadcast_to(as_row(square_sum), (8, slots))
            spread(*sq_net)
        if c == 1:
            loads[2].wait()
            loads[3].wait()
        if c >= 1:
            pass_on(*row_net[c - 1])
        if c >= 2:
            project(c - 2)

    pass_on(*row_net[chunks - 1])
    pass_on(*sq_net)
    project(chunks - 2)
    complete(*sq_net)
    square_pair[0] = jnp.sum(squares[...], axis=0)
    other = {"side": 1 - side}
    pair_copies = [
        remote(square_pair.at[0], square_pair.at[1], pair_send.at[2], pair_recv.at[2], other),
        remote(pair_out.at[0], pair_in.at[0], pair_send.at[0], pair_recv.at[0], other),
        remote(pair_out.at[1], pair_in.at[1], pair_send.at[1], pair_recv.at[1], other),
    ]
    pair_copies[0].start()
    project(chunks - 1)
    pair_out[0] = gate_acc[...].astype(BF16)
    pair_copies[1].start()
    pair_out[1] = up_acc[...].astype(BF16)
    pair_copies[2].start()
    pair_copies[0].wait_recv()
    all_squares = square_pair[0] + square_pair[1]
    inverse = as_column(lax.rsqrt(all_squares[0:1, :] / (2 * half) + 1e-06))
    pair_copies[1].wait_recv()
    gate = (gate_acc[...] + pair_in[0].astype(F32)) * inverse
    gate = gate / (1.0 + jnp.exp(-gate))
    pair_copies[2].wait_recv()
    hidden = (gate * ((up_acc[...] + pair_in[1].astype(F32)) * inverse)).astype(BF16)
    loads[4].wait()

    far, near = pl.ds(1, line - 1), pl.ds(0, 1)
    x_copies = [
        [
            remote(
                x_out.at[c, blocks],
                x_in.at[c, blocks],
                x_send.at[c, i],
                x_recv.at[c, i],
                {"ranks": across},
            )
            for i, blocks in enumerate((far, near))
        ]
        for c in range(chunks)
    ]
    z_copies = [
        [
            remote(
                z_out.at[c, dz - 1],
                z_in.at[c, dz - 1],
                z_send.at[c, dz - 1],
                z_recv.at[c, dz - 1],
                {"ranks": rank_at(dz)},
            )
            for dz in range(1, line)
        ]
        for c in range(chunks)
    ]

    def column_part(c):
        cols = slice(c * width, (c + 1) * width)
        result = dot(hidden, wd_ref[:, cols]) * my_share
        part[c] = result.reshape(ranks, merged, width)
        for dz in range(line):
            there = lax.rem(z + dz, line) * COLUMNS + (1 - x)
            x_out[c, dz] = part[c, there].astype(BF16)
        x_copies[c][0].start()

    for c in range(min(SUM_WINDOW, chunks)):
        column_part(c)
    for c in range(chunks):
        x_copies[c][0].wait_recv()
        if c + SUM_WINDOW < chunks:
            column_part(c + SUM_WINDOW)
        if c == max(0, chunks - 1 - SUM_WINDOW):
            for last in range(chunks):
                x_copies[last][1].start()
        for dz in range(1, line):
            z_out[c, dz - 1] = (part[c, rank_at(dz)] + x_in[c, dz].astype(F32)).astype(BF16)
            z_copies[c][dz - 1].start()
    stores = []
    for c in range(chunks):
        cols = slice(c * width, (c + 1) * width)
        x_copies[c][1].wait_recv()
        expert_out = part[c, me] + x_in[c, 0].astype(F32)
        for dz in range(1, line):
            z_copies[c][dz - 1].wait_recv()
            expert_out = expert_out + z_in[c, dz - 1].astype(F32)
        out_ref[:, cols] = (
            summed[:, cols] + split_dot(members, expert_out, ((0,), (0,)))
        ).astype(BF16)
        store = pltpu.make_async_copy(
            out_ref.at[:, pl.ds(c * width, width)],
            out_hbm.at[:, pl.ds(c * width, width)],
            out_sem.at[c],
        )
        store.start()
        stores.append(store)

    for c in range(chunks):
        finish(*kv_net[c])
        finish(*row_net[c])
        for copy in x_copies[c]:
            copy.wait_send()
        for copy in z_copies[c]:
            copy.wait_send()
    finish(*misc_net)
    finish(*sq_net)
    for copy in pair_copies:
        copy.wait_send()
    for store in stores:
        store.wait()


def fused(
    queries,
    keys,
    values,
    residual,
    merge_map,
    expert_ids,
    gate_weights,
    norm_gain,
    w_gate,
    w_up,
    w_down,
):
    ranks = lax.axis_size("ranks")
    tokens, half = queries.shape
    merged = keys.shape[0]
    hidden = w_gate.shape[2]
    chunks = half // CHUNK
    line = ranks // COLUMNS
    slots = ranks * merged
    anywhere = pl.BlockSpec(memory_space=pl.ANY)
    dma = pltpu.SemaphoreType.DMA
    hops = 2 * line - 1
    return pl.pallas_call(
        functools.partial(layer_kernel, ranks, chunks),
        out_shape=jax.ShapeDtypeStruct((tokens, half), BF16),
        in_specs=[anywhere] * 11,
        out_specs=anywhere,
        scratch_shapes=[
            pltpu.VMEM((merged, half), BF16),
            pltpu.VMEM((merged, half), BF16),
            pltpu.VMEM((1, tokens), jnp.int32),
            pltpu.VMEM((TOP, merged), jnp.int32),
            pltpu.VMEM((TOP, merged), F32),
            pltpu.VMEM((half // HEAD_DIM, HEAD_DIM), BF16),
            pltpu.VMEM((tokens, half), BF16),
            pltpu.VMEM((tokens, half), BF16),
            pltpu.VMEM((half, hidden), BF16),
            pltpu.VMEM((half, hidden), BF16),
            pltpu.VMEM((hidden, half), BF16),
            pltpu.VMEM((tokens, half), BF16),
            pltpu.VMEM((ranks, chunks, 2 * merged, CHUNK), BF16),
            pltpu.VMEM((ranks, chunks, merged, CHUNK), BF16),
            pltpu.VMEM((ranks, 8, slots), F32),
            pltpu.VMEM((ranks, 8, slots), F32),
            pltpu.VMEM((2, 8, slots), F32),
            pltpu.VMEM((tokens, half), F32),
            pltpu.VMEM((slots, hidden), F32),
            pltpu.VMEM((slots, hidden), F32),
            pltpu.VMEM((2, slots, hidden), BF16),
            pltpu.VMEM((2, slots, hidden), BF16),
            pltpu.VMEM((chunks, ranks, merged, CHUNK), F32),
            pltpu.VMEM((chunks, line, merged, CHUNK), BF16),
            pltpu.VMEM((chunks, line, merged, CHUNK), BF16),
            pltpu.VMEM((chunks, line - 1, merged, CHUNK), BF16),
            pltpu.VMEM((chunks, line - 1, merged, CHUNK), BF16),
            dma((11,)),
            dma((chunks,)),
            dma((chunks, hops)),
            dma((chunks, hops)),
            dma((chunks, hops)),
            dma((chunks, hops)),
            dma((hops,)),
            dma((hops,)),
            dma((hops,)),
            dma((hops,)),
            dma((3,)),
            dma((3,)),
            dma((chunks, 2)),
            dma((chunks, 2)),
            dma((chunks, line - 1)),
            dma((chunks, line - 1)),
        ],
        compiler_params=pltpu.CompilerParams(
            collective_id=0, has_side_effects=True, vmem_limit_bytes=60 * 1024 * 1024
        ),
    )(
        queries,
        residual,
        keys,
        values,
        merge_map.reshape(1, tokens),
        expert_ids.T,
        gate_weights.T,
        norm_gain.reshape(half // HEAD_DIM, HEAD_DIM),
        w_gate[0],
        w_up[0],
        w_down[0],
    )


def layer(*arrays):
    ranks = lax.axis_size("ranks")
    merged, half = arrays[1].shape
    dense = 4 * merged // (ranks // 2) >= merged and ranks >= 4
    if dense and half % CHUNK == 0 and half // CHUNK >= 2:
        return fused(*arrays)
    return local(*arrays)


def solution(mesh):
    return jax.shard_map(
        layer,
        mesh=mesh,
        in_specs=(
            P(("groups", "ranks"), "side"),
            P(("groups", "ranks"), "side"),
            P(("groups", "ranks"), "side"),
            P(("groups", "ranks"), "side"),
            P(("groups", "ranks")),
            P(("groups", "ranks"), None),
            P(("groups", "ranks"), None),
            P("side"),
            P("ranks", "side", None),
            P("ranks", "side", None),
            P("ranks", None, "side"),
        ),
        out_specs=P(("groups", "ranks"), "side"),
        check_vma=False,
    )
```
